256 devices in a mesh: tm: 32 (over x, z_lo, core), tensor: 8 (over y, z_hi).
Axes of the slice: x: 4, y: 4, z: 8 (z_hi: 2, z_lo: 4; z = z_hi * 4 + z_lo), core: 2. Of those that a mesh axis runs over, the one named last changes fastest.
Arguments:
- hidden_state: bfloat16 [32, 384, 3072], P('tm')
- base_latent: float32 [384, 64], P('tensor'), may hold values from -6 to 6
- w_modulation: bfloat16 [256, 9216], replicated, may hold values from -1 to 1
- w_up: bfloat16 [3072, 6144], P('tm', 'tensor'), may hold values from -0.109375 to 0.109375
- w_down: bfloat16 [6144, 3072], P('tensor', 'tm'), may hold values from -0.078125 to 0.078125
- w_out: bfloat16 [3072, 64], replicated, may hold values from -0.109375 to 0.109375
- times: int32 [32], P('tm'), may hold values from 0 to 999
- sched_index: int32 [32], P('tm'), may hold values from 0 to 999
- slide_count: int32 [1], replicated, may hold values from 1 to 31
Outputs:
- new_latents: float32 [32, 384, 64], P('tm', 'tensor')
The draws below stay inside these ranges and needn't reach their ends.
All inputs are finite; a program needn't handle non-finite values.
Results may differ from the reference program's by a relative error of at most 0.002.
Values may be sent and summed in bfloat16 or wider, within the bound.
A program may use at most 64 MiB of HBM per device.

```python
import math
import jax
import jax.numpy as jnp
from jax import lax

D = 3072
FF = 6144
LAT = 64
TEMB = 256
SCHED = 1000
TOK = 384
STEPS = 32


def draw_hidden_state(key, part):
    key = jax.random.fold_in(key, 11)
    key_base, key_cols, key_rows = jax.random.split(key, 3)
    columns = jnp.exp(jax.random.uniform(key_cols, (D,), jnp.float32, -1.15, 1.15))
    rowscale = jnp.exp(jax.random.uniform(key_rows, (STEPS, TOK, 1), jnp.float32, -1.15, 1.15))
    values = jax.random.normal(key_base, (STEPS, TOK, D), jnp.float32)
    return (values * columns * rowscale).astype(jnp.bfloat16)


def touch_ends(result, key, smallest, high):
    longest = result.shape.index(max(result.shape))
    spots = []
    for shift in (0, 1):
        where = [jax.random.randint(jax.random.fold_in(key, axis), (), 0, length) for axis, length in enumerate(result.shape)]
        where[longest] = (where[longest] + shift) % result.shape[longest]
        spots.append(tuple(where))
    return result.at[spots[0]].set(smallest).at[spots[1]].set(high)


def level_of(rng, shape, cuts, smallest, high):
    level = 1.0
    for dim, blocks in cuts:
        steps = jax.random.uniform(jax.random.fold_in(jax.random.fold_in(rng, 6), dim), (blocks,), jnp.float32, smallest / len(cuts), high / len(cuts))
        level = level * jnp.repeat(jnp.exp(steps), shape[dim] // blocks).reshape((-1,) + (1,) * (len(shape) - 1 - dim))
    return level


def noise(key, extent, deviation, bound, shards=(), kind=jnp.bfloat16):
    level = level_of(key, extent, shards, -0.22, 0.18) if shards else 1.0
    drawn = jax.random.normal(key, extent, jnp.float32) * deviation * level
    return jnp.minimum(jnp.maximum(drawn, -bound), bound).astype(kind)


def setup_inputs(seed: int = 0) -> dict:
    seeds = jax.random.split(jax.random.key(seed), 10)
    return {
        "hidden_state": draw_hidden_state(jax.random.fold_in(seeds[9], 71), 0),
        "base_latent": noise(seeds[1], (TOK, LAT), 1.0, 6.0, ((0, 8),), jnp.float32),
        "w_modulation": noise(seeds[2], (TEMB, 3 * D), (TEMB // 9) ** -0.5, 1.0),
        "w_up": noise(seeds[3], (D, FF), D ** -0.5, 0.109375, ((0, 32), (1, 8))),
        "w_down": noise(seeds[4], (FF, D), FF ** -0.5, 0.078125, ((0, 8), (1, 32))),
        "w_out": noise(seeds[5], (D, LAT), D ** -0.5, 0.109375),
        "times": touch_ends(jax.random.randint(seeds[6], (STEPS,), 0, SCHED), jax.random.fold_in(seeds[6], 1), 0, SCHED - 1).astype(jnp.int32),
        "sched_index": touch_ends(jax.random.randint(seeds[7], (STEPS,), 0, SCHED), jax.random.fold_in(seeds[7], 1), 0, SCHED - 1).astype(jnp.int32),
        "slide_count": jax.random.randint(seeds[8], (1,), 1, STEPS).astype(jnp.int32),
    }


def modulation(times, w_modulation):
    half = TEMB // 2
    freqs = jnp.exp(-math.log(10000.0) * jnp.arange(half, dtype=jnp.float32) / half)
    angles = times.astype(jnp.float32)[:, None] * freqs[None, :]
    embed = jnp.concatenate([jnp.cos(angles), jnp.sin(angles)], axis=1)
    cond = jax.nn.silu(embed).astype(jnp.bfloat16)
    return jnp.dot(cond, w_modulation, preferred_element_type=jnp.float32)

def reference(hidden_state, base_latent, w_modulation, w_up, w_down, w_out, times, sched_index, slide_count):
    mods = modulation(times, w_modulation)
    head = w_out.astype(jnp.float32)

    def one_step(pair):
        hidden, modrow = pair
        shift = modrow[:D]
        scale = modrow[D:2 * D]
        gate = modrow[2 * D:]
        values = hidden.astype(jnp.float32)
        center = lax.optimization_barrier(jnp.mean(values, axis=-1, keepdims=True))
        spread = lax.optimization_barrier(jnp.mean((values - center) ** 2, axis=-1, keepdims=True))
        normed = ((values - center) * lax.rsqrt(spread + 1e-06) * (1.0 + scale) + shift).astype(jnp.bfloat16)
        active = jax.nn.gelu(jnp.dot(normed, w_up, preferred_element_type=jnp.float32), approximate=True).astype(jnp.bfloat16)
        mixed = jnp.dot(active, w_down, preferred_element_type=jnp.float32)
        block_out = values + gate * mixed
        return jnp.dot(block_out, head, precision=lax.Precision.HIGHEST)
    drift = lax.map(one_step, (hidden_state, mods))
    step_size = 0.1 + 0.3 * sched_index.astype(jnp.float32) / SCHED
    reached = base_latent[None] + jnp.cumsum(step_size[:, None, None] * drift, axis=0)
    picked = jnp.minimum(jnp.arange(STEPS, dtype=jnp.int32) + slide_count[0] - 1, STEPS - 1).astype(jnp.int32)
    return jnp.take(reached, picked, axis=0)
```

```python
import functools
import math

import jax
import jax.numpy as jnp
import numpy as np
from jax import lax
from jax.experimental import pallas as pl
from jax.experimental.pallas import tpu as pltpu
from jax.sharding import PartitionSpec as P

SCHED = 1000
D, FFB, LAT, TEMB, TOK = 3072, 768, 64, 256, 384
HALF = FFB // 2
ROWS = 192
F32, BF16 = jnp.float32, jnp.bfloat16
NT = (((1,), (1,)), ((), ()))


def nt_dot(a, b):
    return lax.dot_general(a, b, NT, preferred_element_type=F32)


def dot(a, b):
    return jnp.dot(a, b, preferred_element_type=F32)


def eye(n):
    i = lax.broadcasted_iota(jnp.int32, (n, n), 0)
    j = lax.broadcasted_iota(jnp.int32, (n, n), 1)
    return jnp.where(i == j, 1.0, 0.0).astype(BF16)


def device(x, zl, c, y, zh):
    return (x * 8 + zl * 2 + c, y * 2 + zh)


def kernel(
    hid_h, base_v, wmod_h, wup_h, wdn_h, wout_h, freq_v, times_s, sched_s, slide_s,
    out_v,
    hid, wmod, wdn, wout, normed, wup, wdg, wdstage, ctile, mods, gch, gbuf, psend, pown, pin,
    w2t, pre, act, head, part, prt, qy, ry, rz, zin, xsend, xin,
    loc, up_s, up_r, dn_s, dn_r, nm_s, nm_r, ct_s, ct_r, zs_own, zs_fwd, zr, xs, xf, xr, xo,
    ps_s, ps_r, pt_s, pt_r, ya_s, ya_r, za_s, za_r, xa_s, xa_r,
):
    tm, te = lax.axis_index("tm"), lax.axis_index("tensor")
    x, zl, c = tm // 8, (tm // 2) % 4, tm % 2
    y, zh = te // 2, te % 2
    place = x * 4 + zl
    partner = device(x, zl, 1 - c, y, zh)
    z = zh * 4 + zl

    def at_x(d, core=c):
        return device((x + d) % 4, zl, core, y, zh)

    def at_zl(zp, core=c):
        return device(x, zp, core, y, zh)

    def at_z(d):
        zp = (z + d) % 8
        return device(x, zp % 4, c, y, zp // 4)

    def at_y(d):
        return device(x, zl, c, (y + d) % 4, zh)

    def send(src, dst, ssem, rsem, dev):
        return pltpu.make_async_remote_copy(
            src_ref=src, dst_ref=dst, send_sem=ssem, recv_sem=rsem,
            device_id=dev, device_id_type=pl.DeviceIdType.MESH,
        )

    barrier = pltpu.get_barrier_semaphore()

    def greet(dev):
        pl.semaphore_signal(barrier, inc=1, device_id=dev, device_id_type=pl.DeviceIdType.MESH)

    greet(partner)
    for d in (1, 2, 3):
        greet(at_x(d))
        greet(at_x(d, 1 - c))
        greet(at_y(d))
        greet(at_zl((zl + d) % 4, 1 - c))
    for d in range(1, 8):
        greet(at_z(d))

    my_rows = pl.ds(pl.multiple_of(place * ROWS + c * 96, 32), 96)
    mine = pl.ds(pl.multiple_of(c * HALF, 128), HALF)
    other = pl.ds(pl.multiple_of((1 - c) * HALF, 128), HALF)
    cp_up = pltpu.make_async_copy(wup_h.at[:, mine], wup.at[my_rows, :], loc.at[0])
    cp_dn = pltpu.make_async_copy(wdn_h, wdn, loc.at[1])
    cp_ss = pltpu.make_async_copy(wmod_h.at[:, : 2 * D], wmod.at[:, : 2 * D], loc.at[2])
    cp_hid = pltpu.make_async_copy(hid_h, hid, loc.at[3])
    cp_gate = pltpu.make_async_copy(wmod_h.at[:, 2 * D :], wmod.at[:, 2 * D :], loc.at[4])
    cp_out = pltpu.make_async_copy(wout_h, wout, loc.at[5])
    for cp in (cp_up, cp_dn, cp_ss, cp_hid, cp_gate, cp_out):
        cp.start()

    t = times_s[0].astype(F32)
    angles = freq_v[...] * t
    emb = jnp.concatenate([jnp.cos(angles), jnp.sin(angles)], axis=1)
    cond = (emb * jax.nn.sigmoid(emb)).astype(BF16).astype(F32)
    step = 0.1 + 0.3 * sched_s[0].astype(F32) / SCHED
    slot = zl * 2 + c
    tile = jnp.concatenate([cond, jnp.full((8, 128), 1.0, F32) * step], axis=1)
    rowid = lax.broadcasted_iota(jnp.int32, (8, TEMB + 128), 0)
    ctile[slot] = jnp.where(rowid == slot, tile, 0.0)
    cond_b = cond.astype(BF16)

    pl.semaphore_wait(barrier, 20)

    up_x = send(wup_h.at[:, other], wup.at[my_rows, :], up_s, up_r, partner)
    up_x.start()
    ct = []
    for d in range(1, 8):
        to = (slot + d) % 8
        ct.append(send(ctile.at[slot], ctile.at[slot], ct_s.at[d], ct_r.at[d], at_zl(to // 2, to % 2)))
        ct[-1].start()

    cp_dn.wait()
    own_half = pl.ds(pl.multiple_of(c * 96, 32), 96)
    wdstage[0] = nt_dot(eye(96), wdn[:HALF, :]).astype(BF16)
    wdstage[1] = nt_dot(eye(96), wdn[HALF:, :]).astype(BF16)
    dn_x = send(wdstage.at[1 - c], wdg.at[x, own_half, :], dn_s, dn_r, partner)
    dn_x.start()
    wdg[x, own_half, :] = wdstage[c]

    m = zl // 2
    zz = zl + m * (3 - 2 * zl)
    order = [k + m * (3 - 2 * k) for k in (zz, 1 - zz, 2, 3)]

    def rows_of(xp, zp, lo=0, n=ROWS):
        return pl.ds(pl.multiple_of((xp * 4 + zp) * ROWS + lo, 32), n)

    def block(xp, k, lo=0, n=ROWS):
        if k == 4:
            return wdg.at[xp, pl.ds(lo, n), :]
        return wup.at[rows_of(xp, order[k], lo, n), :]

    left, right, far = (x + 3) % 4, (x + 1) % 4, (x + 2) % 4

    def x_out(k):
        return [
            send(block(x, k), block(x, k), xs.at[k, 0], xr.at[k, 0], at_x(1)),
            send(block(x, k), block(x, k), xs.at[k, 1], xr.at[k, 1], at_x(3)),
        ]

    def x_fwd(k):
        return [
            send(block(left, k, 0, 96), block(left, k, 0, 96), xf.at[k, 0], xo.at[k, 0], at_x(1)),
            send(block(right, k, 96, 96), block(right, k, 96, 96), xf.at[k, 1], xo.at[k, 1], at_x(3)),
        ]

    def x_start(k):
        for cp in x_out(k):
            cp.start()

    def x_relay(k):
        send(block(left, k), block(left, k), xs.at[k, 0], xr.at[k, 0], at_x(1)).wait_recv()
        fw = x_fwd(k)
        fw[0].start()
        send(block(right, k), block(right, k), xs.at[k, 1], xr.at[k, 1], at_x(3)).wait_recv()
        fw[1].start()

    def x_last(k):
        send(block(far, k, 0, 96), block(far, k, 0, 96), xf.at[k, 0], xo.at[k, 0], at_x(1)).wait_recv()
        send(block(far, k, 96, 96), block(far, k, 96, 96), xf.at[k, 1], xo.at[k, 1], at_x(3)).wait_recv()

    def z_send(k, ssem, to):
        return send(block(x, k), block(x, k), ssem, zr.at[order[k]], at_zl(to))

    def z_fwd(k, act_on):
        zp = order[k]

        @pl.when(jnp.logical_and(zp < zl, zl < 3))
        def _():
            act_on(z_send(k, zs_fwd.at[k], zl + 1))

        @pl.when(jnp.logical_and(zp > zl, zl > 0))
        def _():
            act_on(z_send(k, zs_fwd.at[k], zl - 1))

    def z_relay(k):
        z_send(k, zs_fwd.at[k], zl).wait_recv()
        z_fwd(k, lambda cp: cp.start())

    def z_own(act_on):
        @pl.when(zl < 3)
        def _():
            act_on(z_send(0, zs_own.at[0], zl + 1))

        @pl.when(zl > 0)
        def _():
            act_on(z_send(0, zs_own.at[1], zl - 1))

    cp_up.wait()
    up_x.wait_recv()
    x_start(0)
    z_own(lambda cp: cp.start())
    dn_x.wait_recv()
    x_start(4)

    cp_ss.wait()

    def mod_cols(i, _):
        cols = pl.ds(pl.multiple_of(i * 512, 512), 512)
        mods[:, cols] = dot(cond_b, wmod[:, cols])
        return 0

    lax.fori_loop(0, 12, mod_cols, 0)
    cp_hid.wait()

    def norm_rows(i, _):
        rows = pl.ds(pl.multiple_of(i * 16, 16), 16)
        v = hid[rows, :].astype(F32)
        mean = jnp.sum(v, axis=1, keepdims=True) * (1.0 / D)
        v = v - mean
        var = jnp.sum(v * v, axis=1, keepdims=True) * (1.0 / D)
        v = v * lax.rsqrt(var + 1e-06)
        v = v * (1.0 + mods[0:1, D:]) + mods[0:1, :D]
        normed[pl.ds(pl.multiple_of(c * TOK + i * 16, 16), 16), :] = v.astype(BF16)
        return 0

    def norm_copy(q):
        rows = pl.ds(pl.multiple_of(c * TOK + q * 96, 32), 96)
        return send(normed.at[rows, :], normed.at[rows, :], nm_s.at[q], nm_r.at[q], partner)

    for q in range(2):
        lax.fori_loop(q * 6, q * 6 + 6, norm_rows, 0)
        norm_copy(q).start()

    z_relay(1)
    x_relay(0)
    x_start(1)
    for q in range(2, 4):
        lax.fori_loop(q * 6, q * 6 + 6, norm_rows, 0)
        norm_copy(q).start()
    x_relay(4)

    cp_out.wait()
    share = pl.ds(pl.multiple_of(te * 384, 128), 384)
    wo = wout[share, :].astype(F32)
    wo = jnp.concatenate([wo, wo], axis=1)
    lane = lax.broadcasted_iota(jnp.int32, (384, 128), 1)
    wo = jnp.where(lane // 64 == c, wo, 0.0).astype(BF16)
    head[...] = dot(hid[:, share], wo)

    for d in range(1, 8):
        frm = (slot + 8 - d) % 8
        send(ctile.at[frm], ctile.at[frm], ct_s.at[d], ct_r.at[d], partner).wait_recv()
    cp_gate.wait()
    cond8 = ctile[0, :, :TEMB]
    for s in range(1, 8):
        cond8 = cond8 + ctile[s, :, :TEMB]
    cond8 = cond8.astype(BF16)
    for i in range(8):
        g = dot(cond8, wmod[:, 2 * D + i * 384 : 2 * D + (i + 1) * 384])
        gch[2 * i] = g[:, :ROWS]
        gch[2 * i + 1] = g[:, ROWS:]
    eye64 = eye(64)

    def gate_head(xp, _):
        p = xp * 4 + zl
        wt = nt_dot(eye64, wout[pl.ds(pl.multiple_of(p * ROWS, 32), ROWS), :])
        for s in range(8):
            g = gch[p, s : s + 1, :] * wt
            hi = g.astype(BF16)
            gbuf[xp, s * 64 : (s + 1) * 64, :] = hi
            gbuf[xp, 512 + s * 64 : 512 + (s + 1) * 64, :] = (g - hi.astype(F32)).astype(BF16)
        return 0

    lax.fori_loop(0, 4, gate_head, 0)

    z_relay(2)
    x_relay(1)
    x_start(2)

    x_last(4)

    def partial(zp, _):
        hi_rows = pl.ds(pl.multiple_of(zp * 128, 128), 128)
        lo_rows = pl.ds(pl.multiple_of(512 + zp * 128, 128), 128)
        acc = jnp.zeros((128, HALF), F32)
        for xp in range(4):
            acc = acc + dot(gbuf[xp, hi_rows, :], wdg[xp]) + dot(gbuf[xp, lo_rows, :], wdg[xp])
        psend[zp] = acc.astype(BF16)

        @pl.when(zp == zl)
        def _():
            pown[...] = acc

        return 0

    lax.fori_loop(0, 4, partial, 0)
    pcopies = []
    for d in (1, 2, 3):
        to = (zl + d) % 4
        pcopies.append(send(psend.at[to], pin.at[zl], ps_s.at[d - 1], ps_r.at[d - 1], at_zl(to)))
        pcopies[-1].start()

    for q in range(4):
        norm_rows_in = pl.ds(pl.multiple_of((1 - c) * TOK + q * 96, 32), 96)
        send(normed.at[norm_rows_in, :], normed.at[norm_rows_in, :], nm_s.at[q], nm_r.at[q], partner).wait_recv()
    x_last(0)
    z_relay(3)
    x_relay(2)
    x_start(3)
    x_last(1)

    def chunk(xp, mm):
        return pl.ds(pl.multiple_of((xp * 2 + mm) * 384, 128), 384)

    def up(xps, mm, first):
        def tile_rows(i, _):
            rows = pl.ds(pl.multiple_of(i * 128, 128), 128)
            acc = None if first else pre[rows, :]
            for xp in xps:
                v = dot(normed[rows, chunk(xp, mm)], wup[chunk(xp, mm), :])
                acc = v if acc is None else acc + v
            pre[rows, :] = acc
            return 0

        lax.fori_loop(0, 6, tile_rows, 0)

    up([x, left, right, far], m, True)
    x_relay(3)
    up([x, left, right], 1 - m, False)

    w2 = pown[...]
    for d in (1, 2, 3):
        frm = (zl + 4 - d) % 4
        send(psend.at[frm], pin.at[frm], ps_s.at[d - 1], ps_r.at[d - 1], at_zl(frm)).wait_recv()
        w2 = w2 + pin[frm].astype(F32)
    hi = w2.astype(BF16)
    lo = (w2 - hi.astype(F32)).astype(BF16)
    w2t[...] = jnp.zeros((256, 768), BF16)
    w2t[0:64, 0:384] = hi[:64]
    w2t[64:128, 384:768] = hi[64:]
    w2t[128:192, 0:384] = lo[:64]
    w2t[192:256, 384:768] = lo[64:]

    lane1 = lax.broadcasted_iota(jnp.int32, (1, 128), 1)
    step0 = jnp.sum(ctile[zl * 2, :, TEMB:], axis=0, keepdims=True)
    step1 = jnp.sum(ctile[zl * 2 + 1, :, TEMB:], axis=0, keepdims=True)
    steps = jnp.where(lane1 < 64, step0, step1)

    x_last(2)
    x_last(3)

    def finish(i, _):
        rows = pl.ds(pl.multiple_of(i * 128, 128), 128)
        for j in range(2):
            jr = pl.ds(pl.multiple_of(j * TOK + i * 128, 128), 128)
            v = pre[jr, :] + dot(normed[jr, chunk(far, 1 - m)], wup[chunk(far, 1 - m), :])
            act[:, j * HALF : (j + 1) * HALF] = jax.nn.gelu(v, approximate=True).astype(BF16)
        r = nt_dot(act[...], w2t[...])
        part[rows, :] = (r[:, :128] + r[:, 128:] + head[rows, :] * 1.0) * steps
        return 0

    lax.fori_loop(0, 3, finish, 0)

    pt = []
    for b in range(8):
        rows = pl.ds(pl.multiple_of(b * 48 + (1 - c) * 24, 8), 24)
        pt.append(send(part.at[rows, :], prt.at[b], pt_s.at[b], pt_r.at[b], partner))
        pt[-1].start()
    for b in range(8):
        pt[b].wait_recv()
        qy[b] = part[pl.ds(pl.multiple_of(b * 48 + c * 24, 8), 24), :] + prt[b]
    ya = []
    for d in (1, 2, 3):
        to = (y + d) % 4
        ya.append(send(qy.at[pl.ds(to * 2, 2)], ry.at[d - 1], ya_s.at[d - 1], ya_r.at[d - 1], at_y(d)))
        ya[-1].start()
    tot = qy[pl.ds(y * 2, 2)]
    for d in (1, 2, 3):
        ya[d - 1].wait_recv()
        tot = tot + ry[d - 1]
    rz[...] = tot
    za = []
    for d in range(1, 8):
        to = (z + d) % 8
        za.append(send(rz.at[to // 4], zin.at[z], za_s.at[d - 1], za_r.at[d - 1], at_z(d)))
        za[-1].start()
    zin[z] = rz[zh]
    for d in range(1, 8):
        frm = (z + 8 - d) % 8
        send(rz.at[0], zin.at[frm], za_s.at[d - 1], za_r.at[d - 1], at_z(d)).wait_recv()
    vs = [zin[i] + zin[4 + i] for i in range(4)]
    slide = slide_s[0]
    lane24 = lax.broadcasted_iota(jnp.int32, (24, 128), 1) // 64
    xa = []

    def prefix(xp, cp):
        last = xp * 8 + zl * 2 + cp + slide - 1
        acc = jnp.zeros((24, 128), F32)
        for i in range(4):
            acc = acc + jnp.where(lane24 + (x * 8 + i * 2) <= last, vs[i], 0.0)
        return acc + pltpu.roll(acc, 64, 1)

    for d in range(4):
        for e in range(2):
            if d == 0 and e == 0:
                continue
            n = d * 2 + e
            core = (c + e) % 2
            xsend[n] = prefix((x + d) % 4, core)
            xa.append((send(xsend.at[n], xin.at[x, c], xa_s.at[n], xa_r.at[n], at_x(d, core)), d, e))
            xa[-1][0].start()
    xin[x, c] = prefix(x, c)
    for cp, d, e in xa:
        send(xsend.at[d * 2 + e], xin.at[(x + 4 - d) % 4, (c + e) % 2], xa_s.at[d * 2 + e], xa_r.at[d * 2 + e], partner).wait_recv()
    for h in range(2):
        s = xin[0, h] + xin[1, h] + xin[2, h] + xin[3, h]
        out_v[h * 24 : (h + 1) * 24, :] = base_v[h * 24 : (h + 1) * 24, :] + s[:, :64]

    up_x.wait_send()
    dn_x.wait_send()
    for cp in ct + pcopies + pt + ya + za:
        cp.wait_send()
    for cp, _, _ in xa:
        cp.wait_send()
    for q in range(4):
        norm_copy(q).wait_send()
    for k in range(5):
        for cp in x_out(k) + x_fwd(k):
            cp.wait_send()
    z_own(lambda cp: cp.wait_send())
    for k in (1, 2, 3):
        z_fwd(k, lambda cp: cp.wait_send())


def body(hidden_state, base_latent, w_modulation, w_up, w_down, w_out, times, sched_index, slide_count):
    half = TEMB // 2
    freqs = np.exp(-math.log(10000.0) * np.arange(half, dtype=np.float32) / half).astype(np.float32)
    freqs = jnp.asarray(np.broadcast_to(freqs, (8, half)))
    any_, vmem, smem = (pl.BlockSpec(memory_space=s) for s in (pl.ANY, pltpu.VMEM, pltpu.SMEM))
    V, dma = pltpu.VMEM, pltpu.SemaphoreType.DMA
    out = pl.pallas_call(
        kernel,
        out_shape=jax.ShapeDtypeStruct((48, LAT), F32),
        in_specs=[any_, vmem, any_, any_, any_, any_, vmem, smem, smem, smem],
        out_specs=vmem,
        scratch_shapes=[
            V((TOK, D), BF16),
            V((TEMB, 3 * D), BF16),
            V((FFB, 96), BF16),
            V((D, LAT), BF16),
            V((2 * TOK, D), BF16),
            V((D, HALF), BF16),
            V((4, ROWS, HALF), BF16),
            V((2, 96, HALF), BF16),
            V((8, 8, TEMB + 128), F32),
            V((8, 2 * D), F32),
            V((16, 8, ROWS), F32),
            V((4, 1024, ROWS), BF16),
            V((4, 128, HALF), BF16),
            V((128, HALF), F32),
            V((4, 128, HALF), BF16),
            V((256, 768), BF16),
            V((2 * TOK, HALF), F32),
            V((128, 2 * HALF), BF16),
            V((TOK, 128), F32),
            V((TOK, 128), F32),
            V((8, 24, 128), F32),
            V((8, 24, 128), F32),
            V((3, 2, 24, 128), F32),
            V((2, 24, 128), F32),
            V((8, 24, 128), F32),
            V((8, 24, 128), F32),
            V((4, 2, 24, 128), F32),
            dma((6,)),
            dma, dma, dma, dma,
            dma((4,)), dma((4,)),
            dma((8,)), dma((8,)),
            dma((2,)), dma((4,)), dma((4,)),
            dma((5, 2)), dma((5, 2)), dma((5, 2)), dma((5, 2)),
            dma((3,)), dma((3,)),
            dma((8,)), dma((8,)),
            dma((3,)), dma((3,)),
            dma((7,)), dma((7,)),
            dma((8,)), dma((8,)),
        ],
        compiler_params=pltpu.CompilerParams(
            collective_id=0, has_side_effects=True, vmem_limit_bytes=48 * 2**20
        ),
        cost_estimate=pl.CostEstimate(flops=4 * 10**9, bytes_accessed=10**7, transcendentals=300000),
        name="picard",
    )(
        hidden_state[0], base_latent, w_modulation, w_up, w_down, w_out, freqs,
        times, sched_index, slide_count,
    )
    return out[None]


def solution(mesh):
    placed = (
        P("tm", None, None),
        P("tensor", None),
        P(),
        P("tm", "tensor"),
        P("tensor", "tm"),
        P(),
        P("tm"),
        P("tm"),
        P(),
    )
    return jax.shard_map(
        body, mesh=mesh, in_specs=placed, out_specs=P("tm", "tensor", None), check_vma=False
    )
```

```python
import functools
import math

import jax
import jax.numpy as jnp
from jax import lax
from jax.experimental import pallas as pl
from jax.experimental.pallas import tpu as pltpu
from jax.sharding import PartitionSpec as P

SCHED = 1000
D, FFB, LAT, TEMB, TOK = 3072, 768, 64, 256, 384
HALF = FFB // 2
ROWS = 192
F32, BF16 = jnp.float32, jnp.bfloat16
NT = (((1,), (1,)), ((), ()))


def nt_dot(a, b):
    return lax.dot_general(a, b, NT, preferred_element_type=F32)


def dot(a, b):
    return jnp.dot(a, b, preferred_element_type=F32)


def device(x, zl, c, y, zh):
    return (x * 8 + zl * 2 + c, y * 2 + zh)


def kernel(
    hid_h, base_h, wmod_h, wup_h, wdn_h, wout_h, times_h, sched_h, slide_h,
    out_v,
    times_s, sched_s, slide_s, hid, wmod, base, wout, normed, wup, wdg, ctile, mods, gch, wch, gbuf, psend, pown, pin,
    w2t, pre, act, head, part, ry, rz, zin, xsend, xin,
    loc, up_s, up_r, dn_s, dn_r, nm_s, nm_r, ct_s, ct_r, zs_own, zs_fwd, zr, xs, xf, xr, xo,
    ps_s, ps_r, ya_s, ya_r, za_s, za_r, xa_s, xa_r,
):
    tm, te = lax.axis_index("tm"), lax.axis_index("tensor")
    x, zl, c = tm // 8, (tm // 2) % 4, tm % 2
    y, zh = te // 2, te % 2
    place = x * 4 + zl
    partner = device(x, zl, 1 - c, y, zh)
    z = zh * 4 + zl

    def at_x(d, core=c):
        return device((x + d) % 4, zl, core, y, zh)

    def at_zl(zp, core=c):
        return device(x, zp, core, y, zh)

    def at_z(d):
        zp = (z + d) % 8
        return device(x, zp % 4, c, y, zp // 4)

    def at_y(d, core=c):
        return device(x, zl, core, (y + d) % 4, zh)

    def send(src, dst, ssem, rsem, dev):
        return pltpu.make_async_remote_copy(
            src_ref=src, dst_ref=dst, send_sem=ssem, recv_sem=rsem,
            device_id=dev, device_id_type=pl.DeviceIdType.MESH,
        )

    barrier = pltpu.get_barrier_semaphore()

    def greet(dev):
        pl.semaphore_signal(barrier, inc=1, device_id=dev, device_id_type=pl.DeviceIdType.MESH)

    greet(partner)
    for d in (1, 2, 3):
        greet(at_x(d))
        greet(at_x(d, 1 - c))
        greet(at_y(d))
        greet(at_y(d, 1 - c))
        greet(at_zl((zl + d) % 4, 1 - c))
    for d in range(1, 8):
        greet(at_z(d))

    my_rows = pl.ds(pl.multiple_of(place * ROWS + c * 96, 32), 96)
    mine = pl.ds(pl.multiple_of(c * HALF, 128), HALF)
    cp_up = pltpu.make_async_copy(wup_h.at[:, mine], wup.at[my_rows, :], loc.at[0])
    own_half = pl.ds(pl.multiple_of(c * 96, 32), 96)
    cp_dn = pltpu.make_async_copy(wdn_h.at[:, mine], wdg.at[x, own_half, :], loc.at[1])
    cp_ss = pltpu.make_async_copy(wmod_h.at[:, : 2 * D], wmod.at[:, : 2 * D], loc.at[2])
    cp_hid = pltpu.make_async_copy(hid_h, hid, loc.at[3])
    cp_gate = pltpu.make_async_copy(wmod_h.at[:, 2 * D :], wmod.at[:, 2 * D :], loc.at[4])
    cp_out = pltpu.make_async_copy(wout_h, wout, loc.at[5])
    cp_base = pltpu.make_async_copy(base_h, base, loc.at[6])
    scalars = [
        pltpu.make_async_copy(a, b, loc.at[7 + i])
        for i, (a, b) in enumerate(((times_h, times_s), (sched_h, sched_s), (slide_h, slide_s)))
    ]
    for cp in scalars:
        cp.start()
    for cp in (cp_up, cp_dn, cp_ss, cp_hid, cp_gate, cp_out, cp_base):
        cp.start()

    for cp in scalars:
        cp.wait()
    t = times_s[0].astype(F32)
    k = lax.broadcasted_iota(jnp.int32, (8, 128), 1).astype(F32)
    angles = jnp.exp(k * (-math.log(10000.0) / 128)) * t
    emb = jnp.concatenate([jnp.cos(angles), jnp.sin(angles)], axis=1)
    cond = (emb * jax.nn.sigmoid(emb)).astype(BF16).astype(F32)
    step = 0.1 + 0.3 * sched_s[0].astype(F32) / SCHED
    slot = zl * 2 + c
    tile = jnp.concatenate([cond, jnp.full((8, 128), 1.0, F32) * step], axis=1)
    rowid = lax.broadcasted_iota(jnp.int32, (8, TEMB + 128), 0)
    ctile[slot] = jnp.where(rowid == slot, tile, 0.0)
    cond_b = cond.astype(BF16)

    pl.semaphore_wait(barrier, 23)

    def own_rows(k, core):
        cols = pl.ds(pl.multiple_of(core * HALF, 128), HALF)
        if k == 4:
            return wdn_h.at[:, cols], wdg.at[x, own_half, :]
        return wup_h.at[:, cols], wup.at[my_rows, :]

    def own_x(k):
        cps = []
        for side in range(2):
            for e in range(2):
                core = (c + e) % 2
                src, dst = own_rows(k, core)
                to = at_x(1 if side == 0 else 3, core)
                cps.append(send(src, dst, xs.at[k, side, e], xr.at[k, side, c], to))
        return cps

    def own_z(act_on):
        for e in range(2):
            core = (c + e) % 2
            src, dst = own_rows(0, core)

            @pl.when(zl < 3)
            def _():
                act_on(send(src, dst, zs_own.at[0, e], zr.at[zl, c], at_zl(zl + 1, core)))

            @pl.when(zl > 0)
            def _():
                act_on(send(src, dst, zs_own.at[1, e], zr.at[zl, c], at_zl(zl - 1, core)))

    def own_core(k, ssem, rsem):
        src, dst = own_rows(k, 1 - c)
        return send(src, dst, ssem, rsem, partner)

    def start(cps):
        for cp in cps:
            cp.start()

    own_z(lambda cp: cp.start())
    start(own_x(0))
    start(own_x(4))
    up_x = own_core(0, up_s, up_r)
    dn_x = own_core(4, dn_s, dn_r)
    start([up_x, dn_x])
    ct = []
    for d in range(1, 8):
        to = (slot + d) % 8
        ct.append(send(ctile.at[slot], ctile.at[slot], ct_s.at[d], ct_r.at[d], at_zl(to // 2, to % 2)))
        ct[-1].start()


    m = zl // 2
    zz = zl + m * (3 - 2 * zl)
    order = [k + m * (3 - 2 * k) for k in (zz, 1 - zz, 2, 3)]

    def rows_of(xp, zp, lo=0, n=ROWS):
        return pl.ds(pl.multiple_of((xp * 4 + zp) * ROWS + lo, 32), n)

    def block(xp, k, lo=0, n=ROWS):
        if k == 4:
            return wdg.at[xp, pl.ds(lo, n), :]
        return wup.at[rows_of(xp, order[k], lo, n), :]

    left, right, far = (x + 3) % 4, (x + 1) % 4, (x + 2) % 4

    def x_half(k, side, h):
        blk = block(x, k, h * 96, 96)
        return send(blk, blk, xs.at[k, side, h], xr.at[k, side, h], at_x(1 if side == 0 else 3))

    def x_out(k):
        return [x_half(k, side, h) for h in range(2) for side in range(2)]

    def x_fwd(k):
        lb, rb = block(left, k, 0, 96), block(right, k, 96, 96)
        return [
            send(lb, lb, xf.at[k, 0], xo.at[k, 0], at_x(1)),
            send(rb, rb, xf.at[k, 1], xo.at[k, 1], at_x(3)),
        ]

    def x_start(k, h):
        x_half(k, h, h).start()
        x_half(k, 1 - h, h).start()

    def x_relay(k):
        fw = x_fwd(k)
        for h, src in enumerate((left, right)):
            blk = block(src, k, h * 96, 96)
            send(blk, blk, xs.at[k, h, h], xr.at[k, h, h], at_x(1)).wait_recv()
            fw[h].start()

    def x_near(k):
        for h, src in enumerate((left, right)):
            blk = block(src, k, 96 - h * 96, 96)
            send(blk, blk, xs.at[k, h, 1 - h], xr.at[k, h, 1 - h], at_x(1)).wait_recv()

    def x_far(k):
        for h in range(2):
            blk = block(far, k, h * 96, 96)
            send(blk, blk, xf.at[k, h], xo.at[k, h], at_x(1)).wait_recv()

    def z_send(k, h, ssem, to):
        blk = block(x, k, h * 96, 96)
        return send(blk, blk, ssem, zr.at[order[k], h], at_zl(to))

    def z_fwd(k, h, act_on):
        zp = order[k]

        @pl.when(jnp.logical_and(zp < zl, zl < 3))
        def _():
            act_on(z_send(k, h, zs_fwd.at[k, h], zl + 1))

        @pl.when(jnp.logical_and(zp > zl, zl > 0))
        def _():
            act_on(z_send(k, h, zs_fwd.at[k, h], zl - 1))

    def z_relay(k, h):
        z_send(k, h, zs_fwd.at[k, h], zl).wait_recv()
        z_fwd(k, h, lambda cp: cp.start())

    def run(*tokens):
        for t in tokens:
            n = [int(v) for v in t[1:]]
            if t[0] == "Z":
                z_relay(*n)
            elif t[0] == "A":
                x_start(*n)
            elif t[0] == "R":
                x_relay(*n)
            elif t[0] == "N":
                x_near(*n)
            elif t[0] == "F":
                x_far(*n)

    cp_ss.wait()

    def mod_cols(i, _):
        cols = pl.ds(pl.multiple_of(i * 512, 512), 512)
        mods[:, cols] = dot(cond_b, wmod[:, cols])
        return 0

    lax.fori_loop(0, 12, mod_cols, 0)
    cp_hid.wait()

    def norm_rows(i, _):
        rows = pl.ds(pl.multiple_of(i * 16, 16), 16)
        v = hid[rows, :].astype(F32)
        mean = jnp.sum(v, axis=1, keepdims=True) * (1.0 / D)
        v = v - mean
        var = jnp.sum(v * v, axis=1, keepdims=True) * (1.0 / D)
        v = v * lax.rsqrt(var + 1e-06)
        v = v * (1.0 + mods[0:1, D:]) + mods[0:1, :D]
        normed[pl.ds(pl.multiple_of(c * TOK + i * 16, 16), 16), :] = v.astype(BF16)
        return 0

    def norm_copy(q):
        rows = pl.ds(pl.multiple_of(c * TOK + q * 96, 32), 96)
        return send(normed.at[rows, :], normed.at[rows, :], nm_s.at[q], nm_r.at[q], partner)

    for q in range(2):
        lax.fori_loop(q * 6, q * 6 + 6, norm_rows, 0)
        norm_copy(q).start()

    run("Z10", "A10", "R0", "Z11", "A11")
    for q in range(2, 4):
        lax.fori_loop(q * 6, q * 6 + 6, norm_rows, 0)
        norm_copy(q).start()
    run("R4")

    cp_out.wait()
    share = pl.ds(pl.multiple_of(te * 384, 128), 384)
    wo = wout[:, share].astype(F32)
    wo = jnp.concatenate([wo, wo], axis=0)
    row = lax.broadcasted_iota(jnp.int32, (128, 384), 0)
    wo = jnp.where(row // 64 == c, wo, 0.0).astype(BF16)
    head[...] = nt_dot(hid[:, share], wo)

    for d in range(1, 8):
        frm = (slot + 8 - d) % 8
        send(ctile.at[frm], ctile.at[frm], ct_s.at[d], ct_r.at[d], partner).wait_recv()
    cp_gate.wait()
    cond8 = ctile[0, :, :TEMB]
    for s in range(1, 8):
        cond8 = cond8 + ctile[s, :, :TEMB]
    cond8 = cond8.astype(BF16)
    for i in range(8):
        g = dot(cond8, wmod[:, 2 * D + i * 384 : 2 * D + (i + 1) * 384])
        gch[2 * i] = g[:, :ROWS]
        gch[2 * i + 1] = g[:, ROWS:]
        wt = wout[:, i * 384 : (i + 1) * 384].astype(F32)
        wch[2 * i] = wt[:, :ROWS]
        wch[2 * i + 1] = wt[:, ROWS:]

    def gate_head(xp, _):
        p = xp * 4 + zl
        wt = wch[p]
        for s in range(8):
            g = gch[p, s : s + 1, :] * wt
            hi = g.astype(BF16)
            gbuf[xp, s * 64 : (s + 1) * 64, :] = hi
            gbuf[xp, 512 + s * 64 : 512 + (s + 1) * 64, :] = (g - hi.astype(F32)).astype(BF16)
        return 0

    lax.fori_loop(0, 4, gate_head, 0)

    run("Z20", "A20", "Z21", "A21", "R1")

    run("Z30", "A30", "Z31", "A31", "N4", "F4")

    def partial(zp, _):
        hi_rows = pl.ds(pl.multiple_of(zp * 128, 128), 128)
        lo_rows = pl.ds(pl.multiple_of(512 + zp * 128, 128), 128)
        acc = jnp.zeros((128, HALF), F32)
        for xp in range(4):
            acc = acc + dot(gbuf[xp, hi_rows, :], wdg[xp]) + dot(gbuf[xp, lo_rows, :], wdg[xp])
        psend[zp] = acc.astype(BF16)

        @pl.when(zp == zl)
        def _():
            pown[...] = acc

        return 0

    cp_dn.wait()
    dn_x.wait_recv()
    lax.fori_loop(0, 4, partial, 0)
    pcopies = []
    for d in (1, 2, 3):
        to = (zl + d) % 4
        pcopies.append(send(psend.at[to], pin.at[zl], ps_s.at[d - 1], ps_r.at[d - 1], at_zl(to)))
        pcopies[-1].start()

    for q in range(4):
        norm_rows_in = pl.ds(pl.multiple_of((1 - c) * TOK + q * 96, 32), 96)
        send(normed.at[norm_rows_in, :], normed.at[norm_rows_in, :], nm_s.at[q], nm_r.at[q], partner).wait_recv()
    run("R2", "N0", "F0", "N1", "F1")

    def chunk(xp, mm):
        return pl.ds(pl.multiple_of((xp * 2 + mm) * 384, 128), 384)

    def up(xps, mm, first):
        def tile_rows(i, _):
            rows = pl.ds(pl.multiple_of(i * 128, 128), 128)
            acc = None if first else pre[rows, :]
            for xp in xps:
                v = dot(normed[rows, chunk(xp, mm)], wup[chunk(xp, mm), :])
                acc = v if acc is None else acc + v
            pre[rows, :] = acc
            return 0

        lax.fori_loop(0, 6, tile_rows, 0)

    cp_up.wait()
    up_x.wait_recv()
    up([x, left, right, far], m, True)
    run("R3", "N2", "N3")
    up([x, left, right], 1 - m, False)

    w2 = pown[...]
    for d in (1, 2, 3):
        frm = (zl + 4 - d) % 4
        send(psend.at[frm], pin.at[frm], ps_s.at[d - 1], ps_r.at[d - 1], at_zl(frm)).wait_recv()
        w2 = w2 + pin[frm].astype(F32)
    hi = w2.astype(BF16)
    lo = (w2 - hi.astype(F32)).astype(BF16)
    w2t[...] = jnp.zeros((256, 768), BF16)
    w2t[0:64, 0:384] = hi[:64]
    w2t[64:128, 384:768] = hi[64:]
    w2t[128:192, 0:384] = lo[:64]
    w2t[192:256, 384:768] = lo[64:]

    lane1 = lax.broadcasted_iota(jnp.int32, (1, 128), 1)
    step0 = jnp.sum(ctile[zl * 2, :, TEMB:], axis=0, keepdims=True)
    step1 = jnp.sum(ctile[zl * 2 + 1, :, TEMB:], axis=0, keepdims=True)
    steps = jnp.where(lane1 < 64, step0, step1)

    run("F2", "F3")

    ya = []
    for d in (2, 1, 3, 0):
        yp = (y + d) % 4
        rows = pl.ds(pl.multiple_of(yp * 96, 32), 96)
        jrows = [pl.ds(pl.multiple_of(j * TOK + yp * 96, 32), 96) for j in range(2)]
        lhs = jnp.concatenate([normed[r, chunk(far, 1 - m)] for r in jrows], axis=0)
        v = dot(lhs, wup[chunk(far, 1 - m), :])
        for j in range(2):
            g = jax.nn.gelu(pre[jrows[j], :] + v[j * 96 : (j + 1) * 96], approximate=True)
            act[:, j * HALF : (j + 1) * HALF] = g.astype(BF16)
        r = nt_dot(act[...], w2t[...])
        tile = (r[:, :128] + r[:, 128:] + head[rows, :]) * steps
        part[yp] = tile.reshape(2, 2, 24, 128)
        for e in range(2):
            if d == 0 and e == 0:
                continue
            core = (c + e) % 2
            n = d * 2 + e
            cp = send(part.at[yp, :, core], ry.at[n], ya_s.at[n], ya_r.at[n], at_y(d, core))
            cp.start()
            ya.append((cp, n))
    tot = part[y, :, c]
    for cp, n in ya:
        cp.wait_recv()
        tot = tot + ry[n]
    rz[...] = tot
    za = []
    for d in range(1, 8):
        to = (z + d) % 8
        za.append(send(rz.at[to // 4], zin.at[z], za_s.at[d - 1], za_r.at[d - 1], at_z(d)))
        za[-1].start()
    zin[z] = rz[zh]
    for d in range(1, 8):
        frm = (z + 8 - d) % 8
        send(rz.at[0], zin.at[frm], za_s.at[d - 1], za_r.at[d - 1], at_z(d)).wait_recv()
    vs = [zin[i] + zin[4 + i] for i in range(4)]
    slide = slide_s[0]
    lane24 = lax.broadcasted_iota(jnp.int32, (24, 128), 1) // 64
    xa = []

    def prefix(xp, cp):
        last = xp * 8 + zl * 2 + cp + slide - 1
        acc = jnp.zeros((24, 128), F32)
        for i in range(4):
            acc = acc + jnp.where(lane24 + (x * 8 + i * 2) <= last, vs[i], 0.0)
        return acc + pltpu.roll(acc, 64, 1)

    for d in range(4):
        for e in range(2):
            if d == 0 and e == 0:
                continue
            n = d * 2 + e
            core = (c + e) % 2
            xsend[n] = prefix((x + d) % 4, core)
            xa.append((send(xsend.at[n], xin.at[x, c], xa_s.at[n], xa_r.at[n], at_x(d, core)), d, e))
            xa[-1][0].start()
    xin[x, c] = prefix(x, c)
    for cp, d, e in xa:
        send(xsend.at[d * 2 + e], xin.at[(x + 4 - d) % 4, (c + e) % 2], xa_s.at[d * 2 + e], xa_r.at[d * 2 + e], partner).wait_recv()
    cp_base.wait()
    for h in range(2):
        s = xin[0, h] + xin[1, h] + xin[2, h] + xin[3, h]
        out_v[h * 24 : (h + 1) * 24, :] = base[h * 24 : (h + 1) * 24, :] + s[:, :64]

    up_x.wait_send()
    dn_x.wait_send()
    for cp in ct + pcopies + za + [t[0] for t in ya + xa]:
        cp.wait_send()
    for q in range(4):
        norm_copy(q).wait_send()
    for k in range(5):
        for cp in (own_x(k) if k in (0, 4) else x_out(k)) + x_fwd(k):
            cp.wait_send()
    own_z(lambda cp: cp.wait_send())
    for h in range(2):
        for k in (1, 2, 3):
            z_fwd(k, h, lambda cp: cp.wait_send())


def body(hidden_state, base_latent, w_modulation, w_up, w_down, w_out, times, sched_index, slide_count):
    hbm = pl.BlockSpec(memory_space=pltpu.HBM)
    V, dma = pltpu.VMEM, pltpu.SemaphoreType.DMA
    out = pl.pallas_call(
        kernel,
        out_shape=jax.ShapeDtypeStruct((48, LAT), F32),
        in_specs=[hbm] * 9,
        out_specs=pl.BlockSpec(memory_space=pltpu.VMEM),
        scratch_shapes=[
            pltpu.SMEM((1,), jnp.int32), pltpu.SMEM((1,), jnp.int32), pltpu.SMEM((1,), jnp.int32),
            V((TOK, D), BF16),
            V((TEMB, 3 * D), BF16),
            V((48, LAT), F32),
            V((LAT, D), BF16),
            V((2 * TOK, D), BF16),
            V((D, HALF), BF16),
            V((4, ROWS, HALF), BF16),
            V((8, 8, TEMB + 128), F32),
            V((8, 2 * D), F32),
            V((16, 8, ROWS), F32),
            V((16, LAT, ROWS), F32),
            V((4, 1024, ROWS), BF16),
            V((4, 128, HALF), BF16),
            V((128, HALF), F32),
            V((4, 128, HALF), BF16),
            V((256, 768), BF16),
            V((2 * TOK, HALF), F32),
            V((96, 2 * HALF), BF16),
            V((TOK, 128), F32),
            V((4, 2, 2, 24, 128), F32),
            V((8, 2, 24, 128), F32),
            V((2, 24, 128), F32),
            V((8, 24, 128), F32),
            V((8, 24, 128), F32),
            V((4, 2, 24, 128), F32),
            dma((10,)),
            dma, dma, dma, dma,
            dma((4,)), dma((4,)),
            dma((8,)), dma((8,)),
            dma((2, 2)), dma((4, 2)), dma((4, 2)),
            dma((5, 2, 2)), dma((5, 2)), dma((5, 2, 2)), dma((5, 2)),
            dma((3,)), dma((3,)),
            dma((8,)), dma((8,)),
            dma((7,)), dma((7,)),
            dma((8,)), dma((8,)),
        ],
        compiler_params=pltpu.CompilerParams(
            collective_id=0, has_side_effects=True, vmem_limit_bytes=56518246
        ),
        cost_estimate=pl.CostEstimate(flops=4 * 10**9, bytes_accessed=10**7, transcendentals=300000),
        name="picard",
    )(
        hidden_state[0], base_latent, w_modulation, w_up, w_down.T, w_out.T,
        times, sched_index, slide_count,
    )
    return out[None]


def solution(mesh):
    placed = (
        P("tm", None, None),
        P("tensor", None),
        P(),
        P("tm", "tensor"),
        P("tensor", "tm"),
        P(),
        P("tm"),
        P("tm"),
        P(),
    )
    return jax.shard_map(
        body, mesh=mesh, in_specs=placed, out_specs=P("tm", "tensor", None), check_vma=False
    )
```

```python
import functools
import math

import jax
import jax.numpy as jnp
from jax import lax
from jax.experimental import pallas as pl
from jax.experimental.pallas import tpu as pltpu
from jax.sharding import PartitionSpec as P

SCHED = 1000
D, FFB, LAT, TEMB, TOK = 3072, 768, 64, 256, 384
HALF = FFB // 2
ROWS = 192
VMEM_BYTES = 56518246
FIRST = (0, 4)
PLAN = (
    "M", "K1", "Q0", "Q1", "K2", "C", "Z10", "A10", "R0", "Z11", "A11", "Q2",
    "Q3", "R4", "H", "G", "Z20", "A20", "Z21", "A21", "R1", "K3", "Z30", "A30",
    "Z31", "A31", "N4", "F4", "W", "R2", "N0", "F0", "N1", "F1", "U1", "R3",
    "N2", "N3", "U2", "V", "F2", "F3",
)
F32, BF16 = jnp.float32, jnp.bfloat16
NT = (((1,), (1,)), ((), ()))


def nt_dot(a, b):
    return lax.dot_general(a, b, NT, preferred_element_type=F32)


def dot(a, b):
    return jnp.dot(a, b, preferred_element_type=F32)


def device(x, zl, c, y, zh):
    return (x * 8 + zl * 2 + c, y * 2 + zh)


def kernel(
    hid_h, base_h, wmod_h, wup_h, wdn_h, wout_h, times_h, sched_h, slide_h,
    out_v,
    times_s, sched_s, slide_s, hid, wmod, base, wout, normed, wup, wdg, ctile, mods, gch, wch, gbuf, psend, pown, pin,
    w2t, pre, act, head, part, ry, rz, zin, xsend, xin,
    loc, up_s, up_r, dn_s, dn_r, nm_s, nm_r, ct_s, ct_r, ready, zs_own, zs_fwd, zr, xs, xf, xr, xo,
    ps_s, ps_r, ya_s, ya_r, za_s, za_r, xa_s, xa_r,
):
    tm, te = lax.axis_index("tm"), lax.axis_index("tensor")
    x, zl, c = tm // 8, (tm // 2) % 4, tm % 2
    y, zh = te // 2, te % 2
    place = x * 4 + zl
    partner = device(x, zl, 1 - c, y, zh)
    z = zh * 4 + zl

    def at_x(d, core=c):
        return device((x + d) % 4, zl, core, y, zh)

    def at_zl(zp, core=c):
        return device(x, zp, core, y, zh)

    def at_z(d, core=c):
        zp = (z + d) % 8
        return device(x, zp % 4, core, y, zp // 4)

    def at_y(d, core=c):
        return device(x, zl, core, (y + d) % 4, zh)

    def send(src, dst, ssem, rsem, dev):
        return pltpu.make_async_remote_copy(
            src_ref=src, dst_ref=dst, send_sem=ssem, recv_sem=rsem,
            device_id=dev, device_id_type=pl.DeviceIdType.MESH,
        )

    barrier = pltpu.get_barrier_semaphore()

    def greet(dev):
        pl.semaphore_signal(barrier, inc=1, device_id=dev, device_id_type=pl.DeviceIdType.MESH)

    greet(partner)
    for core in (c, 1 - c):
        for d in (1, 3):
            greet(at_x(d, core))
            greet(at_y(d, core))
        for d in (1, 7):
            greet(at_z(d, core))

    my_rows = pl.ds(pl.multiple_of(place * ROWS + c * 96, 32), 96)
    mine = pl.ds(pl.multiple_of(c * HALF, 128), HALF)
    cp_up = pltpu.make_async_copy(wup_h.at[:, mine], wup.at[my_rows, :], loc.at[0])
    own_half = pl.ds(pl.multiple_of(c * 96, 32), 96)
    cp_dn = pltpu.make_async_copy(wdn_h.at[:, mine], wdg.at[x, own_half, :], loc.at[1])
    cp_ss = pltpu.make_async_copy(wmod_h.at[:, : 2 * D], wmod.at[:, : 2 * D], loc.at[2])
    cp_hid = pltpu.make_async_copy(hid_h, hid, loc.at[3])
    cp_gate = pltpu.make_async_copy(wmod_h.at[:, 2 * D :], wmod.at[:, 2 * D :], loc.at[4])
    cp_out = pltpu.make_async_copy(wout_h, wout, loc.at[5])
    cp_base = pltpu.make_async_copy(base_h, base, loc.at[6])
    scalars = [
        pltpu.make_async_copy(a, b, loc.at[7 + i])
        for i, (a, b) in enumerate(((times_h, times_s), (sched_h, sched_s), (slide_h, slide_s)))
    ]
    for cp in scalars:
        cp.start()
    for cp in (cp_up, cp_dn, cp_ss, cp_hid, cp_gate, cp_out, cp_base):
        cp.start()

    for cp in scalars:
        cp.wait()
    t = times_s[0].astype(F32)
    k = lax.broadcasted_iota(jnp.int32, (8, 128), 1).astype(F32)
    angles = jnp.exp(k * (-math.log(10000.0) / 128)) * t
    emb = jnp.concatenate([jnp.cos(angles), jnp.sin(angles)], axis=1)
    cond = (emb * jax.nn.sigmoid(emb)).astype(BF16).astype(F32)
    step = 0.1 + 0.3 * sched_s[0].astype(F32) / SCHED
    slot = zl * 2 + c
    ctile[slot] = jnp.concatenate([cond[:1], jnp.full((1, 128), 1.0, F32) * step], axis=1)
    cond_b = cond.astype(BF16)

    pl.semaphore_wait(barrier, 13)

    def tell(n, dev):
        pl.semaphore_signal(ready.at[n], inc=1, device_id=dev, device_id_type=pl.DeviceIdType.MESH)

    def hear(n):
        pl.semaphore_wait(ready.at[n], 2)
        if n < 3:
            tell(n + 1, at_z(1))
            tell(n + 1, at_z(7))

    tell(0, at_y(3))
    tell(1, at_z(1))
    tell(1, at_z(7))

    def own_rows(k, core):
        cols = pl.ds(pl.multiple_of(core * HALF, 128), HALF)
        if k == 4:
            return wdn_h.at[:, cols], wdg.at[x, own_half, :]
        return wup_h.at[:, cols], wup.at[my_rows, :]

    def own_x(k):
        cps = []
        for side in range(2):
            for e in range(2):
                core = (c + e) % 2
                src, dst = own_rows(k, core)
                to = at_x(1 if side == 0 else 3, core)
                cps.append(send(src, dst, xs.at[k, side, e], xr.at[k, side, c], to))
        return cps

    def own_z(act_on):
        for e in range(2):
            core = (c + e) % 2
            src, dst = own_rows(0, core)

            @pl.when(zl < 3)
            def _():
                act_on(send(src, dst, zs_own.at[0, e], zr.at[zl, c], at_zl(zl + 1, core)))

            @pl.when(zl > 0)
            def _():
                act_on(send(src, dst, zs_own.at[1, e], zr.at[zl, c], at_zl(zl - 1, core)))

    def own_core(k, ssem, rsem):
        src, dst = own_rows(k, 1 - c)
        return send(src, dst, ssem, rsem, partner)

    def start(cps):
        for cp in cps:
            cp.start()

    own_z(lambda cp: cp.start())
    for k in FIRST:
        start(own_x(k))
    up_x = own_core(0, up_s, up_r)
    dn_x = own_core(4, dn_s, dn_r)
    start([up_x, dn_x])
    ct_x = send(ctile.at[slot], ctile.at[slot], ct_s.at[0], ct_r.at[0], partner)
    ct_x.start()
    ct = []

    def share_cond():
        frm = zl * 2 + 1 - c
        send(ctile.at[frm], ctile.at[frm], ct_s.at[0], ct_r.at[0], partner).wait_recv()
        pair = ctile.at[pl.ds(zl * 2, 2)]
        for d in (1, 2, 3):
            ct.append(send(pair, pair, ct_s.at[d], ct_r.at[d], at_zl((zl + d) % 4)))
            ct[-1].start()

    m = zl // 2
    zz = zl + m * (3 - 2 * zl)
    order = [k + m * (3 - 2 * k) for k in (zz, 1 - zz, 2, 3)]

    def rows_of(xp, zp, lo=0, n=ROWS):
        return pl.ds(pl.multiple_of((xp * 4 + zp) * ROWS + lo, 32), n)

    def block(xp, k, lo=0, n=ROWS):
        if k == 4:
            return wdg.at[xp, pl.ds(lo, n), :]
        return wup.at[rows_of(xp, order[k], lo, n), :]

    left, right, far = (x + 3) % 4, (x + 1) % 4, (x + 2) % 4

    def x_half(k, side, h):
        blk = block(x, k, h * 96, 96)
        return send(blk, blk, xs.at[k, side, h], xr.at[k, side, h], at_x(1 if side == 0 else 3))

    def x_out(k):
        return [x_half(k, side, h) for h in range(2) for side in range(2)]

    def x_fwd(k):
        lb, rb = block(left, k, 0, 96), block(right, k, 96, 96)
        return [
            send(lb, lb, xf.at[k, 0], xo.at[k, 0], at_x(1)),
            send(rb, rb, xf.at[k, 1], xo.at[k, 1], at_x(3)),
        ]

    def x_start(k, h):
        x_half(k, h, h).start()
        x_half(k, 1 - h, h).start()

    def x_relay(k):
        fw = x_fwd(k)
        for h, src in enumerate((left, right)):
            blk = block(src, k, h * 96, 96)
            send(blk, blk, xs.at[k, h, h], xr.at[k, h, h], at_x(1)).wait_recv()
            fw[h].start()

    def x_near(k):
        for h, src in enumerate((left, right)):
            blk = block(src, k, 96 - h * 96, 96)
            send(blk, blk, xs.at[k, h, 1 - h], xr.at[k, h, 1 - h], at_x(1)).wait_recv()

    def x_far(k):
        for h in range(2):
            blk = block(far, k, h * 96, 96)
            send(blk, blk, xf.at[k, h], xo.at[k, h], at_x(1)).wait_recv()

    def z_send(k, h, ssem, to):
        blk = block(x, k, h * 96, 96)
        return send(blk, blk, ssem, zr.at[order[k], h], at_zl(to))

    def z_fwd(k, h, act_on):
        zp = order[k]

        @pl.when(jnp.logical_and(zp < zl, zl < 3))
        def _():
            act_on(z_send(k, h, zs_fwd.at[k, h], zl + 1))

        @pl.when(jnp.logical_and(zp > zl, zl > 0))
        def _():
            act_on(z_send(k, h, zs_fwd.at[k, h], zl - 1))

    def z_relay(k, h):
        z_send(k, h, zs_fwd.at[k, h], zl).wait_recv()
        z_fwd(k, h, lambda cp: cp.start())

    def mod_cols(i, _):
        cols = pl.ds(pl.multiple_of(i * 512, 512), 512)
        mods[:, cols] = dot(cond_b, wmod[:, cols])
        return 0

    def modulate():
        cp_ss.wait()
        lax.fori_loop(0, 12, mod_cols, 0)
        cp_hid.wait()

    def norm_rows(i, _):
        rows = pl.ds(pl.multiple_of(i * 16, 16), 16)
        v = hid[rows, :].astype(F32)
        mean = jnp.sum(v, axis=1, keepdims=True) * (1.0 / D)
        v = v - mean
        var = jnp.sum(v * v, axis=1, keepdims=True) * (1.0 / D)
        v = v * lax.rsqrt(var + 1e-06)
        v = v * (1.0 + mods[0:1, D:]) + mods[0:1, :D]
        normed[pl.ds(pl.multiple_of(c * TOK + i * 16, 16), 16), :] = v.astype(BF16)
        return 0

    def norm_copy(q):
        rows = pl.ds(pl.multiple_of(c * TOK + q * 96, 32), 96)
        return send(normed.at[rows, :], normed.at[rows, :], nm_s.at[q], nm_r.at[q], partner)

    def norm(q):
        lax.fori_loop(q * 6, q * 6 + 6, norm_rows, 0)
        norm_copy(q).start()

    def head_share():
        cp_out.wait()
        share = pl.ds(pl.multiple_of(te * 384, 128), 384)
        wo = wout[:, share].astype(F32)
        wo = jnp.concatenate([wo, wo], axis=0)
        row = lax.broadcasted_iota(jnp.int32, (128, 384), 0)
        wo = jnp.where(row // 64 == c, wo, 0.0).astype(BF16)
        head[...] = nt_dot(hid[:, share], wo)

    def gate_head(xp, _):
        p = xp * 4 + zl
        wt = wch[p]
        for s in range(8):
            g = gch[p, s : s + 1, :] * wt
            hi = g.astype(BF16)
            gbuf[xp, s * 64 : (s + 1) * 64, :] = hi
            gbuf[xp, 512 + s * 64 : 512 + (s + 1) * 64, :] = (g - hi.astype(F32)).astype(BF16)
        return 0

    def gates():
        for d in (1, 2, 3):
            pair = ctile.at[pl.ds((zl + 4 - d) % 4 * 2, 2)]
            send(pair, pair, ct_s.at[d], ct_r.at[d], partner).wait_recv()
        cp_gate.wait()
        row8 = lax.broadcasted_iota(jnp.int32, (8, TEMB), 0)
        cond8 = jnp.zeros((8, TEMB), F32)
        for s in range(8):
            cond8 = jnp.where(row8 == s, ctile[s, :, :TEMB], cond8)
        cond8 = cond8.astype(BF16)
        for i in range(8):
            g = dot(cond8, wmod[:, 2 * D + i * 384 : 2 * D + (i + 1) * 384])
            gch[2 * i] = g[:, :ROWS]
            gch[2 * i + 1] = g[:, ROWS:]
            wt = wout[:, i * 384 : (i + 1) * 384].astype(F32)
            wch[2 * i] = wt[:, :ROWS]
            wch[2 * i + 1] = wt[:, ROWS:]
        lax.fori_loop(0, 4, gate_head, 0)

    def partial(zp, _):
        hi_rows = pl.ds(pl.multiple_of(zp * 128, 128), 128)
        lo_rows = pl.ds(pl.multiple_of(512 + zp * 128, 128), 128)
        acc = jnp.zeros((128, HALF), F32)
        for xp in range(4):
            acc = acc + dot(gbuf[xp, hi_rows, :], wdg[xp]) + dot(gbuf[xp, lo_rows, :], wdg[xp])
        psend[zp] = acc.astype(BF16)

        @pl.when(zp == zl)
        def _():
            pown[...] = acc

        return 0

    pcopies = []

    def fold():

        cp_dn.wait()
        dn_x.wait_recv()
        lax.fori_loop(0, 4, partial, 0)
        for d in (1, 2, 3):
            to = (zl + d) % 4
            pcopies.append(send(psend.at[to], pin.at[zl], ps_s.at[d - 1], ps_r.at[d - 1], at_zl(to)))
            pcopies[-1].start()

    def chunk(xp, mm):
        return pl.ds(pl.multiple_of((xp * 2 + mm) * 384, 128), 384)

    def up(xps, mm, first):
        def tile_rows(i, _):
            rows = pl.ds(pl.multiple_of(i * 128, 128), 128)
            acc = None if first else pre[rows, :]
            for xp in xps:
                v = dot(normed[rows, chunk(xp, mm)], wup[chunk(xp, mm), :])
                acc = v if acc is None else acc + v
            pre[rows, :] = acc
            return 0

        lax.fori_loop(0, 6, tile_rows, 0)

    def up_first():
        for q in range(4):
            norm_rows_in = pl.ds(pl.multiple_of((1 - c) * TOK + q * 96, 32), 96)
            send(normed.at[norm_rows_in, :], normed.at[norm_rows_in, :], nm_s.at[q], nm_r.at[q], partner).wait_recv()
        cp_up.wait()
        up_x.wait_recv()
        up([x, left, right, far], m, True)

    def up_second():
        up([x, left, right], 1 - m, False)

    def collect():
        w2 = pown[...]
        for d in (1, 2, 3):
            frm = (zl + 4 - d) % 4
            send(psend.at[frm], pin.at[frm], ps_s.at[d - 1], ps_r.at[d - 1], at_zl(frm)).wait_recv()
            w2 = w2 + pin[frm].astype(F32)
        hi = w2.astype(BF16)
        lo = (w2 - hi.astype(F32)).astype(BF16)
        w2t[...] = jnp.zeros((256, 768), BF16)
        w2t[0:64, 0:384] = hi[:64]
        w2t[64:128, 384:768] = hi[64:]
        w2t[128:192, 0:384] = lo[:64]
        w2t[192:256, 384:768] = lo[64:]

    work = {
        "M": modulate, "Q0": norm, "Q1": norm, "Q2": norm, "Q3": norm, "H": head_share,
        "C": share_cond, "K1": hear, "K2": hear, "K3": hear, "G": gates, "W": fold, "U1": lambda _: up_first(), "U2": lambda _: up_second(), "V": collect,
    }

    def run(*tokens):
        for t in tokens:
            n = [int(v) for v in t[1:]]
            if t[0] == "Z":
                z_relay(*n)
            elif t in work:
                work[t](*n)
            elif t[0] == "A":
                x_start(*n)
            elif t[0] == "R":
                x_relay(*n)
            elif t[0] == "N":
                x_near(*n)
            elif t[0] == "F":
                x_far(*n)

    run(*PLAN)

    lane1 = lax.broadcasted_iota(jnp.int32, (1, 128), 1)
    step0 = ctile[zl * 2, :, TEMB:]
    step1 = ctile[zl * 2 + 1, :, TEMB:]
    steps = jnp.where(lane1 < 64, step0, step1)

    pl.semaphore_wait(ready.at[0], 1)
    ya = []
    for d in (2, 1, 3, 0):
        yp = (y + d) % 4
        rows = pl.ds(pl.multiple_of(yp * 96, 32), 96)
        jrows = [pl.ds(pl.multiple_of(j * TOK + yp * 96, 32), 96) for j in range(2)]
        lhs = jnp.concatenate([normed[r, chunk(far, 1 - m)] for r in jrows], axis=0)
        v = dot(lhs, wup[chunk(far, 1 - m), :])
        for j in range(2):
            g = jax.nn.gelu(pre[jrows[j], :] + v[j * 96 : (j + 1) * 96], approximate=True)
            act[:, j * HALF : (j + 1) * HALF] = g.astype(BF16)
        r = nt_dot(act[...], w2t[...])
        tile = (r[:, :128] + r[:, 128:] + head[rows, :]) * steps
        part[yp] = tile.reshape(2, 2, 24, 128)
        for e in range(2):
            if d == 0 and e == 0:
                continue
            core = (c + e) % 2
            n = d * 2 + e
            cp = send(part.at[yp, :, core], ry.at[n], ya_s.at[n], ya_r.at[n], at_y(d, core))
            cp.start()
            ya.append((cp, n))
    tot = part[y, :, c]
    for cp, n in ya:
        cp.wait_recv()
        tot = tot + ry[n]
    rz[...] = tot
    za = []
    for d in range(1, 8):
        to = (z + d) % 8
        za.append(send(rz.at[to // 4], zin.at[z], za_s.at[d - 1], za_r.at[d - 1], at_z(d)))
        za[-1].start()
    zin[z] = rz[zh]
    for d in range(1, 8):
        frm = (z + 8 - d) % 8
        send(rz.at[0], zin.at[frm], za_s.at[d - 1], za_r.at[d - 1], at_z(d)).wait_recv()
    vs = [zin[i] + zin[4 + i] for i in range(4)]
    slide = slide_s[0]
    lane24 = lax.broadcasted_iota(jnp.int32, (24, 128), 1) // 64
    xa = []

    def prefix(xp, cp):
        last = xp * 8 + zl * 2 + cp + slide - 1
        acc = jnp.zeros((24, 128), F32)
        for i in range(4):
            acc = acc + jnp.where(lane24 + (x * 8 + i * 2) <= last, vs[i], 0.0)
        return acc + pltpu.roll(acc, 64, 1)

    for d in range(4):
        for e in range(2):
            if d == 0 and e == 0:
                continue
            n = d * 2 + e
            core = (c + e) % 2
            xsend[n] = prefix((x + d) % 4, core)
            xa.append((send(xsend.at[n], xin.at[x, c], xa_s.at[n], xa_r.at[n], at_x(d, core)), d, e))
            xa[-1][0].start()
    xin[x, c] = prefix(x, c)
    for cp, d, e in xa:
        send(xsend.at[d * 2 + e], xin.at[(x + 4 - d) % 4, (c + e) % 2], xa_s.at[d * 2 + e], xa_r.at[d * 2 + e], partner).wait_recv()
    cp_base.wait()
    for h in range(2):
        s = xin[0, h] + xin[1, h] + xin[2, h] + xin[3, h]
        out_v[h * 24 : (h + 1) * 24, :] = base[h * 24 : (h + 1) * 24, :] + s[:, :64]

    ct_x.wait_send()
    up_x.wait_send()
    dn_x.wait_send()
    for cp in ct + pcopies + za + [t[0] for t in ya + xa]:
        cp.wait_send()
    for q in range(4):
        norm_copy(q).wait_send()
    for k in range(5):
        for cp in (own_x(k) if k in (0, 4) else x_out(k)) + x_fwd(k):
            cp.wait_send()
    own_z(lambda cp: cp.wait_send())
    for h in range(2):
        for k in (1, 2, 3):
            z_fwd(k, h, lambda cp: cp.wait_send())


def body(hidden_state, base_latent, w_modulation, w_up, w_down, w_out, times, sched_index, slide_count):
    hbm = pl.BlockSpec(memory_space=pltpu.HBM)
    V, dma = pltpu.VMEM, pltpu.SemaphoreType.DMA
    out = pl.pallas_call(
        kernel,
        out_shape=jax.ShapeDtypeStruct((48, LAT), F32),
        in_specs=[hbm] * 9,
        out_specs=pl.BlockSpec(memory_space=pltpu.VMEM),
        scratch_shapes=[
            pltpu.SMEM((1,), jnp.int32), pltpu.SMEM((1,), jnp.int32), pltpu.SMEM((1,), jnp.int32),
            V((TOK, D), BF16),
            V((TEMB, 3 * D), BF16),
            V((48, LAT), F32),
            V((LAT, D), BF16),
            V((2 * TOK, D), BF16),
            V((D, HALF), BF16),
            V((4, ROWS, HALF), BF16),
            V((8, 1, TEMB + 128), F32),
            V((8, 2 * D), F32),
            V((16, 8, ROWS), F32),
            V((16, LAT, ROWS), F32),
            V((4, 1024, ROWS), BF16),
            V((4, 128, HALF), BF16),
            V((128, HALF), F32),
            V((4, 128, HALF), BF16),
            V((256, 768), BF16),
            V((2 * TOK, HALF), F32),
            V((96, 2 * HALF), BF16),
            V((TOK, 128), F32),
            V((4, 2, 2, 24, 128), F32),
            V((8, 2, 24, 128), F32),
            V((2, 24, 128), F32),
            V((8, 24, 128), F32),
            V((8, 24, 128), F32),
            V((4, 2, 24, 128), F32),
            dma((10,)),
            dma, dma, dma, dma,
            dma((4,)), dma((4,)),
            dma((4,)), dma((4,)),
            pltpu.SemaphoreType.REGULAR((4,)),
            dma((2, 2)), dma((4, 2)), dma((4, 2)),
            dma((5, 2, 2)), dma((5, 2)), dma((5, 2, 2)), dma((5, 2)),
            dma((3,)), dma((3,)),
            dma((8,)), dma((8,)),
            dma((7,)), dma((7,)),
            dma((8,)), dma((8,)),
        ],
        compiler_params=pltpu.CompilerParams(
            collective_id=0, has_side_effects=True, vmem_limit_bytes=VMEM_BYTES
        ),
        cost_estimate=pl.CostEstimate(flops=4 * 10**9, bytes_accessed=10**7, transcendentals=300000),
        name="picard",
    )(
        hidden_state[0], base_latent, w_modulation, w_up, w_down.T, w_out.T,
        times, sched_index, slide_count,
    )
    return out[None]


def solution(mesh):
    placed = (
        P("tm", None, None),
        P("tensor", None),
        P(),
        P("tm", "tensor"),
        P("tensor", "tm"),
        P(),
        P("tm"),
        P("tm"),
        P(),
    )
    return jax.shard_map(
        body, mesh=mesh, in_specs=placed, out_specs=P("tm", "tensor", None), check_vma=False
    )
```
